32 devices in a mesh: groups: 2 (over x), dp: 2 (over core), feat: 8 (over z, y).
Axes of the slice: x: 2, y: 2, z: 4, core: 2. Of those that a mesh axis runs over, the one named last changes fastest.
Arguments:
- tokens: bfloat16 [8192, 16384], P(('groups', 'dp'), 'feat'), parts along dimension 0, may hold values from -6 to 6
- block_weights: bfloat16 [24, 2048, 13312], P('feat'), may hold values from -0.078125 to 0.078125
- low_in: bfloat16 [16384, 256], P('feat'), may hold values from -0.046875 to 0.046875
- low_out: bfloat16 [256, 106496], P(None, 'feat'), may hold values from -0.375 to 0.375
Outputs:
- hidden: bfloat16 [8192, 53248], P(('groups', 'dp'), 'feat'), parts along dimension 0
The draws below stay inside these ranges and needn't reach their ends.
There are 2 independent parts, one for each index of `groups`. The reference program is written for one: setup_inputs(seed, part) draws one part's arguments, and reference() takes and returns one part's arrays. A program takes and returns all parts, laid end to end along the dimension named above; an argument that names none is the same for every part. Nothing has to cross between parts.
All inputs are finite; a program needn't handle non-finite values.
Results may differ from the reference program's by a relative error of at most 0.005.
Values may be sent and summed in bfloat16 or wider, within the bound.
No kernel may reach another device: no remote copies, remote signals or barrier semaphores. Data moves between devices by JAX's collectives and lax.ppermute only.
A program may use at most 704 MiB of HBM per device.

```python
import jax
import jax.numpy as jnp
from jax import lax

D = 16384
FF = 53248
RANK = 256
BIT_A = 0
BIT_B = 2
TOKENS = 4096
N_FEAT = 8


def levels(own_key, dims, split, least, top_value):
    loudness = 1.0
    for axis_at, shards_of in split:
        steps = jax.random.uniform(jax.random.fold_in(jax.random.fold_in(own_key, 6), axis_at), (shards_of,), jnp.float32, least / len(split), top_value / len(split))
        loudness = loudness * jnp.repeat(jnp.exp(steps), dims[axis_at] // shards_of).reshape((-1,) + (1,) * (len(dims) - 1 - axis_at))
    return loudness


def normal_values(key, dims, scale, reach, cuts=(), kind=jnp.bfloat16):
    entries = jax.random.normal(key, dims, jnp.float32) * scale
    if len(cuts) > 0:
        entries = levels(key, dims, cuts, -0.22, 0.18) * entries
    return jnp.clip(entries, min=-reach, max=reach).astype(kind)


def setup_inputs(seed: int = 0, part: int = 0) -> dict:
    seeds = jax.random.split(jax.random.key(seed), 5)
    own_keys = jax.random.split(jax.random.fold_in(seeds[4], part), 5)
    return {
        "tokens": normal_values(own_keys[0], (TOKENS, D), 1.0, 6.0, ((0, 2), (1, 8))),
        "block_weights": normal_values(seeds[1], (3 * N_FEAT, D // N_FEAT, 2 * FF // N_FEAT), (3 * D // N_FEAT) ** -0.5, 0.078125, ((0, 8),)),
        "low_in": normal_values(seeds[2], (D, RANK), D ** -0.5, 0.046875, ((0, 8),)),
        "low_out": normal_values(seeds[3], (RANK, 2 * FF), RANK ** -0.5, 0.375, ((1, 8),)),
    }


def reference(tokens, block_weights, low_in, low_out):
    tok_count = tokens.shape[0]
    shard_width = block_weights.shape[1]
    col_width = block_weights.shape[2]
    half_width = col_width // 2
    latent = jnp.dot(tokens, low_in, preferred_element_type=jnp.float32).astype(jnp.bfloat16)
    pieces = tokens.reshape(tok_count, N_FEAT, shard_width).transpose(1, 0, 2)
    out_blocks = low_out.reshape(RANK, N_FEAT, col_width).transpose(1, 0, 2)
    weight_blocks = block_weights.reshape(N_FEAT, 3, shard_width, col_width)

    def one_shard(shard_index):
        combined = jnp.dot(latent, out_blocks[shard_index], preferred_element_type=jnp.float32)
        for slot_index, bit_shift in enumerate((-1, BIT_A, BIT_B)):
            if bit_shift < 0:
                source = shard_index
            else:
                source = jnp.bitwise_xor(shard_index, jnp.int32(1 << bit_shift))
            combined = combined + jnp.dot(pieces[source], weight_blocks[shard_index, slot_index], preferred_element_type=jnp.float32)
        gate_part = combined[:, :half_width]
        up_part = combined[:, half_width:]
        return (jax.nn.silu(gate_part) * up_part).astype(jnp.bfloat16)

    result = lax.map(one_shard, jnp.arange(N_FEAT, dtype=jnp.int32))
    return result.transpose(1, 0, 2).reshape(tok_count, N_FEAT * half_width)
```

```python
import functools

import jax
import jax.numpy as jnp
from jax import lax
from jax.experimental import pallas as pl
from jax.experimental.pallas import tpu as pltpu
from jax.sharding import PartitionSpec as P

BIT_A = 0
BIT_B = 2
VMEM_LIMIT = 56 * 1024 * 1024
FIRST_ROWS, HEAD_ROWS, SECOND_ROWS = 9, 2, 5


def from_partner(array, axis, apart):
    return lax.ppermute(array, axis, [(i, i ^ 1 << apart) for i in range(lax.axis_size(axis))])


def plain(tokens, block_weights, low_in, low_out):
    half_width = block_weights.shape[2] // 2
    near_part = from_partner(tokens, "feat", BIT_A)
    far_part = from_partner(tokens, "feat", BIT_B)
    partial_latent = jnp.dot(tokens, low_in, preferred_element_type=jnp.float32)
    latent = lax.psum(partial_latent, "feat").astype(jnp.bfloat16)
    low_part = jnp.dot(latent, low_out, preferred_element_type=jnp.float32)
    combined = low_part + jnp.dot(tokens, block_weights[0], preferred_element_type=jnp.float32)
    combined = combined + jnp.dot(near_part, block_weights[1], preferred_element_type=jnp.float32)
    combined = combined + jnp.dot(far_part, block_weights[2], preferred_element_type=jnp.float32)
    gate_part = combined[:, :half_width]
    up_part = combined[:, half_width:]
    return (jax.nn.silu(gate_part) * up_part).astype(jnp.bfloat16)


def row_cuts(rows, most):
    parts = -(-rows // most)
    while rows % parts or rows // parts % 16:
        parts += 1
    return [(k * (rows // parts), rows // parts) for k in range(parts)]


def product_kernel(plan, *refs):
    tile, pieces, terms, low, add, gated, sends = plan
    refs = list(refs)
    take = lambda count: [refs.pop(0) for _ in range(count)]
    factors = [(take(len(pieces)), take(2)) for _ in range(terms)]
    if low:
        factors.append((take(1), take(2)))
    total_ref = take(1)[0] if add else None
    sent_sem = refs.pop() if sends else None
    sent_refs = refs[len(refs) - len(sends):]
    out_ref = refs[len(refs) - len(sends) - 1]
    copies = [
        pltpu.make_async_copy(factors[0][0][0].at[pl.ds(first, size), :], sent_refs[k], sent_sem.at[k])
        for k, (first, size) in enumerate(sends)
    ]
    if copies:
        @pl.when(pl.program_id(0) == 0)
        def _():
            for copy in copies:
                copy.start()

    cuts = []
    for k, rows in enumerate(pieces):
        cuts += [(k, sum(pieces[:k]), first, size) for first, size in row_cuts(rows, 288 if gated else 512)]
    for piece, before, first, size in cuts:
        here = pl.ds(before + first, size)
        halves = []
        for k in range(2):
            value = None
            for x_refs, weight_refs in factors:
                x = x_refs[0][here, :] if len(x_refs) == 1 else x_refs[piece][pl.ds(first, size), :]
                term = jnp.dot(x, weight_refs[k][...], preferred_element_type=jnp.float32)
                value = term if value is None else value + term
            if add:
                value = value + total_ref[here, k * tile:(k + 1) * tile]
            halves.append(value)
        if gated:
            gate, up = halves
            out_ref[here, :] = (gate / (1.0 + jnp.exp(-gate)) * up).astype(out_ref.dtype)
        else:
            for k in range(2):
                out_ref[here, k * tile:(k + 1) * tile] = halves[k]
    if copies:
        @pl.when(pl.program_id(0) == pl.num_programs(0) - 1)
        def _():
            for copy in copies:
                copy.wait()


def product(tile, factors, weights, low=None, total=None, total_at=0, hidden=None, sends=None, cheaper=1):
    pieces = tuple(piece.shape[0] for piece in factors[0][0])
    rows, depth = sum(pieces), weights.shape[1]
    width = weights.shape[2]
    tiles = width // 2 // tile
    once = pl.Buffered(1)
    operands, in_specs = [], []
    for x, slot in factors:
        operands += [*x, weights, weights]
        in_specs += [pl.BlockSpec(piece.shape, lambda j: (0, 0), pipeline_mode=once) for piece in x]
        in_specs += [
            pl.BlockSpec((None, depth, tile), lambda j, slot=slot: (slot, 0, j)),
            pl.BlockSpec((None, depth, tile), lambda j, slot=slot: (slot, 0, j + tiles)),
        ]
    span = depth * len(factors)
    if low is not None:
        latent, latent_at, low_out = low
        rank = low_out.shape[0]
        operands += [latent, low_out, low_out]
        in_specs += [
            pl.BlockSpec((pl.Element(rows), pl.Element(rank)), lambda j: (latent_at, 0), pipeline_mode=once),
            pl.BlockSpec((rank, tile), lambda j: (0, j)),
            pl.BlockSpec((rank, tile), lambda j: (0, j + tiles)),
        ]
        span += rank
    moved = (rows + width) * span * 2
    aliases = {}
    if total is not None:
        if hidden is None:
            aliases = {len(operands): 0}
        operands.append(total)
        in_specs.append(pl.BlockSpec((pl.Element(rows), pl.Element(2 * tile)), lambda j: (total_at, j * 2 * tile)))
        moved += rows * width * 4
    if hidden is not None:
        all_rows, first, so_far = hidden
        if so_far is not None:
            aliases = {len(operands): 0}
            operands.append(so_far)
            in_specs.append(pl.BlockSpec(memory_space=pl.ANY))
        out_shape = [jax.ShapeDtypeStruct((all_rows, width // 2), jnp.bfloat16)]
        out_specs = [pl.BlockSpec((pl.Element(rows), pl.Element(tile)), lambda j: (first, j * tile))]
        moved += rows * width
    else:
        out_shape = [jax.ShapeDtypeStruct((rows if total is None else total.shape[0], width), jnp.float32)]
        out_specs = [pl.BlockSpec((pl.Element(rows), pl.Element(2 * tile)), lambda j: (total_at, j * 2 * tile))]
        moved += rows * width * 4
    scratch = []
    for _, size in sends or ():
        out_shape.append(jax.ShapeDtypeStruct((size, depth), weights.dtype))
        out_specs.append(pl.BlockSpec(memory_space=pl.ANY))
        scratch = [pltpu.SemaphoreType.DMA((len(sends),))]
    plan = (tile, pieces, len(factors), low is not None, total is not None, hidden is not None, sends or ())
    found = pl.pallas_call(
        functools.partial(product_kernel, plan),
        grid=(tiles,),
        in_specs=in_specs,
        out_specs=out_specs,
        out_shape=out_shape,
        scratch_shapes=scratch,
        input_output_aliases=aliases,
        compiler_params=pltpu.CompilerParams(vmem_limit_bytes=VMEM_LIMIT),
        cost_estimate=pl.CostEstimate(
            flops=2 * rows * span * width // cheaper, bytes_accessed=moved // cheaper, transcendentals=0 if hidden is None else rows * width // 2
        ),
    )(*operands)
    return found if sends else found[0]


def after(value, earlier):
    return lax.optimization_barrier((value, earlier))


def shards(tile, tokens, block_weights, low_in, low_out):
    rows = tokens.shape[0]
    count = lax.axis_size("feat")
    cut = rows * FIRST_ROWS // 16
    head, mid = rows * HEAD_ROWS // 16, rows * SECOND_ROWS // 16
    mix = functools.partial(product, tile, weights=block_weights)

    early_rows = lax.slice_in_dim(tokens, 0, cut)
    near_early = from_partner(early_rows, "feat", BIT_A)
    late_rows, _ = after(lax.slice_in_dim(tokens, cut, rows), early_rows)
    far_late = from_partner(late_rows, "feat", BIT_B)
    tokens, late_rows = after(tokens, late_rows)
    far_head = from_partner(lax.slice_in_dim(tokens, 0, head), "feat", BIT_B)
    partial = jnp.dot(tokens, low_in, preferred_element_type=jnp.float32)
    late_rows, partial = after(late_rows, partial)
    near_late = from_partner(late_rows, "feat", BIT_A)

    sides = [[i for i in range(count) if (i >> BIT_B & 1) == side] for side in range(2)]
    latent = lax.psum_scatter(partial, "feat", scatter_dimension=0, axis_index_groups=sides, tiled=True)

    total, held_a, held_b = mix([([tokens], 0)], sends=[(head, mid - head), (mid, cut - mid)])
    (latent, near_early), total = after((latent, near_early), total)
    across = from_partner(latent.astype(jnp.bfloat16), "feat", BIT_B)

    total = mix([([near_early], 1)], total=total, cheaper=16)
    (across, near_late, far_head, held_a, held_b), total = after((across, near_late, far_head, held_a, held_b), total)
    latent = (latent + across.astype(jnp.float32)).astype(jnp.bfloat16)
    held_a, latent = after(held_a, latent)
    far_a = from_partner(held_a, "feat", BIT_B)
    latent = lax.all_gather(latent, "feat", axis=0, axis_index_groups=sides, tiled=True)

    total = mix([([near_late], 1)], total=total, total_at=cut, cheaper=16)
    (latent, held_b), total = after((latent, held_b), total)
    far_b = from_partner(held_b, "feat", BIT_B)

    hidden = mix([([far_late], 2)], low=(latent, cut, low_out), total=total, total_at=cut, hidden=(rows, cut, None), cheaper=16)
    hidden = mix([([far_head, far_a], 2)], low=(latent, 0, low_out), total=total, hidden=(rows, 0, hidden))
    return mix([([far_b], 2)], low=(latent, mid, low_out), total=total, total_at=mid, hidden=(rows, mid, hidden))


def solution(mesh):
    in_specs = (
        P(("groups", "dp"), "feat"),
        P("feat", None, None),
        P("feat", None),
        P(None, "feat"),
    )
    out_specs = P(("groups", "dp"), "feat")

    def hidden(tokens, block_weights, low_in, low_out):
        count = mesh.shape["feat"]
        rows = tokens.shape[0] // (mesh.shape["groups"] * mesh.shape["dp"])
        half_width = block_weights.shape[2] // 2
        tile = next((t for t in (512, 256, 128) if half_width % t == 0), 0)
        fits = tile and rows % 256 == 0 and rows <= 2048 and block_weights.shape[1] <= 2048 and block_weights.shape[1] % 128 == 0
        fits = fits and count & (count - 1) == 0 and count > 1 << BIT_B and rows % count == 0 and BIT_A < BIT_B and low_in.shape[1] % 128 == 0
        body = functools.partial(shards, tile) if fits else plain
        return jax.shard_map(body, mesh=mesh, in_specs=in_specs, out_specs=out_specs, check_vma=False)(
            tokens, block_weights, low_in, low_out
        )

    return hidden
```

```python
import functools

import jax
import jax.numpy as jnp
from jax import lax
from jax.experimental import pallas as pl
from jax.experimental.pallas import tpu as pltpu
from jax.sharding import PartitionSpec as P

BIT_A = 0
BIT_B = 2
VMEM_LIMIT = 56 * 1024 * 1024
FIRST_ROWS, HEAD_ROWS, SECOND_ROWS = 18, 3, 10


def from_partner(array, axis, apart):
    return lax.ppermute(array, axis, [(i, i ^ 1 << apart) for i in range(lax.axis_size(axis))])


def plain(tokens, block_weights, low_in, low_out):
    half_width = block_weights.shape[2] // 2
    near_part = from_partner(tokens, "feat", BIT_A)
    far_part = from_partner(tokens, "feat", BIT_B)
    partial_latent = jnp.dot(tokens, low_in, preferred_element_type=jnp.float32)
    latent = lax.psum(partial_latent, "feat").astype(jnp.bfloat16)
    low_part = jnp.dot(latent, low_out, preferred_element_type=jnp.float32)
    combined = low_part + jnp.dot(tokens, block_weights[0], preferred_element_type=jnp.float32)
    combined = combined + jnp.dot(near_part, block_weights[1], preferred_element_type=jnp.float32)
    combined = combined + jnp.dot(far_part, block_weights[2], preferred_element_type=jnp.float32)
    gate_part = combined[:, :half_width]
    up_part = combined[:, half_width:]
    return (jax.nn.silu(gate_part) * up_part).astype(jnp.bfloat16)


def row_cuts(rows, most):
    parts = -(-rows // most)
    while rows % parts or rows // parts % 16:
        parts += 1
    return [(k * (rows // parts), rows // parts) for k in range(parts)]


def product_kernel(plan, *refs):
    tile, pieces, terms, low, add, gated, sends = plan
    refs = list(refs)
    take = lambda count: [refs.pop(0) for _ in range(count)]
    factors = [(take(len(pieces)), take(2)) for _ in range(terms)]
    if low:
        factors.append((take(1), take(2)))
    total_ref = take(1)[0] if add else None
    sent_sem = refs.pop() if sends else None
    sent_refs = refs[len(refs) - len(sends):]
    out_ref = refs[len(refs) - len(sends) - 1]
    copies = [
        pltpu.make_async_copy(factors[0][0][0].at[pl.ds(first, size), :], sent_refs[k], sent_sem.at[k])
        for k, (first, size) in enumerate(sends)
    ]
    if copies:
        @pl.when(pl.program_id(0) == 0)
        def _():
            for copy in copies:
                copy.start()

    cuts = []
    for k, rows in enumerate(pieces):
        cuts += [(k, sum(pieces[:k]), first, size) for first, size in row_cuts(rows, 288 if gated else 512)]
    for piece, before, first, size in cuts:
        here = pl.ds(before + first, size)
        halves = []
        for k in range(2):
            value = None
            for x_refs, weight_refs in factors:
                x = x_refs[0][here, :] if len(x_refs) == 1 else x_refs[piece][pl.ds(first, size), :]
                term = jnp.dot(x, weight_refs[k][...], preferred_element_type=jnp.float32)
                value = term if value is None else value + term
            if add:
                value = value + total_ref[here, k * tile:(k + 1) * tile]
            halves.append(value)
        if gated:
            gate, up = halves
            out_ref[here, :] = (gate / (1.0 + jnp.exp(-gate)) * up).astype(out_ref.dtype)
        else:
            for k in range(2):
                out_ref[here, k * tile:(k + 1) * tile] = halves[k]
    if copies:
        @pl.when(pl.program_id(0) == pl.num_programs(0) - 1)
        def _():
            for copy in copies:
                copy.wait()


def product(tile, factors, weights, low=None, total=None, total_at=0, hidden=None, sends=None, cheaper=1):
    pieces = tuple(piece.shape[0] for piece in factors[0][0])
    rows, depth = sum(pieces), weights.shape[1]
    width = weights.shape[2]
    tiles = width // 2 // tile
    once = pl.Buffered(1)
    operands, in_specs = [], []
    for x, slot in factors:
        operands += [*x, weights, weights]
        in_specs += [pl.BlockSpec(piece.shape, lambda j: (0, 0), pipeline_mode=once) for piece in x]
        in_specs += [
            pl.BlockSpec((None, depth, tile), lambda j, slot=slot: (slot, 0, j)),
            pl.BlockSpec((None, depth, tile), lambda j, slot=slot: (slot, 0, j + tiles)),
        ]
    span = depth * len(factors)
    if low is not None:
        latent, latent_at, low_out = low
        rank = low_out.shape[0]
        operands += [latent, low_out, low_out]
        in_specs += [
            pl.BlockSpec((pl.Element(rows), pl.Element(rank)), lambda j: (latent_at, 0), pipeline_mode=once),
            pl.BlockSpec((rank, tile), lambda j: (0, j)),
            pl.BlockSpec((rank, tile), lambda j: (0, j + tiles)),
        ]
        span += rank
    moved = (rows + width) * span * 2
    aliases = {}
    if total is not None:
        if hidden is None:
            aliases = {len(operands): 0}
        operands.append(total)
        in_specs.append(pl.BlockSpec((pl.Element(rows), pl.Element(2 * tile)), lambda j: (total_at, j * 2 * tile)))
        moved += rows * width * 4
    if hidden is not None:
        all_rows, first, so_far = hidden
        if so_far is not None:
            aliases = {len(operands): 0}
            operands.append(so_far)
            in_specs.append(pl.BlockSpec(memory_space=pl.ANY))
        out_shape = [jax.ShapeDtypeStruct((all_rows, width // 2), jnp.bfloat16)]
        out_specs = [pl.BlockSpec((pl.Element(rows), pl.Element(tile)), lambda j: (first, j * tile))]
        moved += rows * width
    else:
        out_shape = [jax.ShapeDtypeStruct((rows if total is None else total.shape[0], width), jnp.float32)]
        out_specs = [pl.BlockSpec((pl.Element(rows), pl.Element(2 * tile)), lambda j: (total_at, j * 2 * tile))]
        moved += rows * width * 4
    scratch = []
    for _, size in sends or ():
        out_shape.append(jax.ShapeDtypeStruct((size, depth), weights.dtype))
        out_specs.append(pl.BlockSpec(memory_space=pl.ANY))
        scratch = [pltpu.SemaphoreType.DMA((len(sends),))]
    plan = (tile, pieces, len(factors), low is not None, total is not None, hidden is not None, sends or ())
    found = pl.pallas_call(
        functools.partial(product_kernel, plan),
        grid=(tiles,),
        in_specs=in_specs,
        out_specs=out_specs,
        out_shape=out_shape,
        scratch_shapes=scratch,
        input_output_aliases=aliases,
        compiler_params=pltpu.CompilerParams(vmem_limit_bytes=VMEM_LIMIT),
        cost_estimate=pl.CostEstimate(
            flops=2 * rows * span * width // cheaper, bytes_accessed=moved // cheaper, transcendentals=0 if hidden is None else rows * width // 2
        ),
    )(*operands)
    return found if sends else found[0]


def after(value, earlier):
    return lax.optimization_barrier((value, earlier))


def shards(tile, tokens, block_weights, low_in, low_out):
    rows = tokens.shape[0]
    count = lax.axis_size("feat")
    cut = rows * FIRST_ROWS // 32
    head, mid = rows * HEAD_ROWS // 32, rows * SECOND_ROWS // 32
    mix = functools.partial(product, tile, weights=block_weights)

    early_rows = lax.slice_in_dim(tokens, 0, cut)
    near_early = from_partner(early_rows, "feat", BIT_A)
    late_rows, _ = after(lax.slice_in_dim(tokens, cut, rows), early_rows)
    far_late = from_partner(late_rows, "feat", BIT_B)
    tokens, late_rows = after(tokens, late_rows)
    far_head = from_partner(lax.slice_in_dim(tokens, 0, head), "feat", BIT_B)
    partial = jnp.dot(tokens, low_in, preferred_element_type=jnp.float32)
    late_rows, partial = after(late_rows, partial)
    near_late = from_partner(late_rows, "feat", BIT_A)

    sides = [[i for i in range(count) if (i >> BIT_B & 1) == side] for side in range(2)]
    latent = lax.psum_scatter(partial, "feat", scatter_dimension=0, axis_index_groups=sides, tiled=True)

    total, held_a, held_b = mix([([tokens], 0)], sends=[(head, mid - head), (mid, cut - mid)])
    (latent, near_early), total = after((latent, near_early), total)
    across = from_partner(latent, "feat", BIT_B)

    total = mix([([near_early], 1)], total=total, cheaper=1000)
    (across, near_late, far_head, held_a, held_b), total = after((across, near_late, far_head, held_a, held_b), total)
    latent = (latent + across).astype(jnp.bfloat16)
    held_a, latent = after(held_a, latent)
    far_a = from_partner(held_a, "feat", BIT_B)
    latent = lax.all_gather(latent, "feat", axis=0, axis_index_groups=sides, tiled=True)

    total = mix([([near_late], 1)], total=total, total_at=cut, cheaper=16)
    (latent, held_b), total = after((latent, held_b), total)
    far_b = from_partner(held_b, "feat", BIT_B)

    hidden = mix([([far_late], 2)], low=(latent, cut, low_out), total=total, total_at=cut, hidden=(rows, cut, None), cheaper=16)
    hidden = mix([([far_head, far_a], 2)], low=(latent, 0, low_out), total=total, hidden=(rows, 0, hidden))
    return mix([([far_b], 2)], low=(latent, mid, low_out), total=total, total_at=mid, hidden=(rows, mid, hidden))


def solution(mesh):
    in_specs = (
        P(("groups", "dp"), "feat"),
        P("feat", None, None),
        P("feat", None),
        P(None, "feat"),
    )
    out_specs = P(("groups", "dp"), "feat")

    def hidden(tokens, block_weights, low_in, low_out):
        count = mesh.shape["feat"]
        rows = tokens.shape[0] // (mesh.shape["groups"] * mesh.shape["dp"])
        half_width = block_weights.shape[2] // 2
        tile = next((t for t in (512, 256, 128) if half_width % t == 0), 0)
        fits = tile and rows % 512 == 0 and rows <= 2048 and block_weights.shape[1] <= 2048 and block_weights.shape[1] % 128 == 0
        fits = fits and count & (count - 1) == 0 and count > 1 << BIT_B and rows % count == 0 and BIT_A < BIT_B and low_in.shape[1] % 128 == 0
        body = functools.partial(shards, tile) if fits else plain
        return jax.shard_map(body, mesh=mesh, in_specs=in_specs, out_specs=out_specs, check_vma=False)(
            tokens, block_weights, low_in, low_out
        )

    return hidden
```

```python
import functools

import jax
import jax.numpy as jnp
from jax import lax
from jax.experimental import pallas as pl
from jax.experimental.pallas import tpu as pltpu
from jax.sharding import PartitionSpec as P

BIT_A = 0
BIT_B = 2
VMEM_LIMIT = 56 * 1024 * 1024
FIRST_ROWS, HEAD_ROWS, SECOND_ROWS = 36, 5, 20


def from_partner(array, axis, apart):
    return lax.ppermute(array, axis, [(i, i ^ 1 << apart) for i in range(lax.axis_size(axis))])


def plain(tokens, block_weights, low_in, low_out):
    half_width = block_weights.shape[2] // 2
    near_part = from_partner(tokens, "feat", BIT_A)
    far_part = from_partner(tokens, "feat", BIT_B)
    partial_latent = jnp.dot(tokens, low_in, preferred_element_type=jnp.float32)
    latent = lax.psum(partial_latent, "feat").astype(jnp.bfloat16)
    low_part = jnp.dot(latent, low_out, preferred_element_type=jnp.float32)
    combined = low_part + jnp.dot(tokens, block_weights[0], preferred_element_type=jnp.float32)
    combined = combined + jnp.dot(near_part, block_weights[1], preferred_element_type=jnp.float32)
    combined = combined + jnp.dot(far_part, block_weights[2], preferred_element_type=jnp.float32)
    gate_part = combined[:, :half_width]
    up_part = combined[:, half_width:]
    return (jax.nn.silu(gate_part) * up_part).astype(jnp.bfloat16)


def row_cuts(rows, most):
    parts = -(-rows // most)
    while rows % parts or rows // parts % 16:
        parts += 1
    return [(k * (rows // parts), rows // parts) for k in range(parts)]


def product_kernel(plan, *refs):
    tile, pieces, terms, low, add, gated, sends = plan
    refs = list(refs)
    take = lambda count: [refs.pop(0) for _ in range(count)]
    factors = [(take(len(pieces)), take(2)) for _ in range(terms)]
    if low:
        factors.append((take(1), take(2)))
    total_ref = take(1)[0] if add else None
    sent_sem = refs.pop() if sends else None
    sent_refs = refs[len(refs) - len(sends):]
    out_ref = refs[len(refs) - len(sends) - 1]
    copies = [
        pltpu.make_async_copy(factors[0][0][0].at[pl.ds(first, size), :], sent_refs[k], sent_sem.at[k])
        for k, (first, size) in enumerate(sends)
    ]
    if copies:
        @pl.when(pl.program_id(0) == 0)
        def _():
            for copy in copies:
                copy.start()

    cuts = []
    for k, rows in enumerate(pieces):
        cuts += [(k, sum(pieces[:k]), first, size) for first, size in row_cuts(rows, 288 if gated else 512)]
    for piece, before, first, size in cuts:
        here = pl.ds(before + first, size)
        halves = []
        for k in range(2):
            value = None
            for x_refs, weight_refs in factors:
                x = x_refs[0][here, :] if len(x_refs) == 1 else x_refs[piece][pl.ds(first, size), :]
                term = jnp.dot(x, weight_refs[k][...], preferred_element_type=jnp.float32)
                value = term if value is None else value + term
            if add:
                value = value + total_ref[here, k * tile:(k + 1) * tile]
            halves.append(value)
        if gated:
            gate, up = halves
            out_ref[here, :] = (gate / (1.0 + jnp.exp(-gate)) * up).astype(out_ref.dtype)
        else:
            for k in range(2):
                out_ref[here, k * tile:(k + 1) * tile] = halves[k]
    if copies:
        @pl.when(pl.program_id(0) == pl.num_programs(0) - 1)
        def _():
            for copy in copies:
                copy.wait()


def product(tile, factors, weights, low=None, total=None, total_at=0, hidden=None, sends=None, cheaper=1):
    pieces = tuple(piece.shape[0] for piece in factors[0][0])
    rows, depth = sum(pieces), weights.shape[1]
    width = weights.shape[2]
    tiles = width // 2 // tile
    once = pl.Buffered(1)
    operands, in_specs = [], []
    for x, slot in factors:
        operands += [*x, weights, weights]
        in_specs += [pl.BlockSpec(piece.shape, lambda j: (0, 0), pipeline_mode=once) for piece in x]
        in_specs += [
            pl.BlockSpec((None, depth, tile), lambda j, slot=slot: (slot, 0, j)),
            pl.BlockSpec((None, depth, tile), lambda j, slot=slot: (slot, 0, j + tiles)),
        ]
    span = depth * len(factors)
    if low is not None:
        latent, latent_at, low_out = low
        rank = low_out.shape[0]
        operands += [latent, low_out, low_out]
        in_specs += [
            pl.BlockSpec((pl.Element(rows), pl.Element(rank)), lambda j: (latent_at, 0), pipeline_mode=once),
            pl.BlockSpec((rank, tile), lambda j: (0, j)),
            pl.BlockSpec((rank, tile), lambda j: (0, j + tiles)),
        ]
        span += rank
    moved = (rows + width) * span * 2
    aliases = {}
    if total is not None:
        if hidden is None:
            aliases = {len(operands): 0}
        operands.append(total)
        in_specs.append(pl.BlockSpec((pl.Element(rows), pl.Element(2 * tile)), lambda j: (total_at, j * 2 * tile)))
        moved += rows * width * 4
    if hidden is not None:
        all_rows, first, so_far = hidden
        if so_far is not None:
            aliases = {len(operands): 0}
            operands.append(so_far)
            in_specs.append(pl.BlockSpec(memory_space=pl.ANY))
        out_shape = [jax.ShapeDtypeStruct((all_rows, width // 2), jnp.bfloat16)]
        out_specs = [pl.BlockSpec((pl.Element(rows), pl.Element(tile)), lambda j: (first, j * tile))]
        moved += rows * width
    else:
        out_shape = [jax.ShapeDtypeStruct((rows if total is None else total.shape[0], width), jnp.float32)]
        out_specs = [pl.BlockSpec((pl.Element(rows), pl.Element(2 * tile)), lambda j: (total_at, j * 2 * tile))]
        moved += rows * width * 4
    scratch = []
    for _, size in sends or ():
        out_shape.append(jax.ShapeDtypeStruct((size, depth), weights.dtype))
        out_specs.append(pl.BlockSpec(memory_space=pl.ANY))
        scratch = [pltpu.SemaphoreType.DMA((len(sends),))]
    plan = (tile, pieces, len(factors), low is not None, total is not None, hidden is not None, sends or ())
    found = pl.pallas_call(
        functools.partial(product_kernel, plan),
        grid=(tiles,),
        in_specs=in_specs,
        out_specs=out_specs,
        out_shape=out_shape,
        scratch_shapes=scratch,
        input_output_aliases=aliases,
        compiler_params=pltpu.CompilerParams(vmem_limit_bytes=VMEM_LIMIT),
        cost_estimate=pl.CostEstimate(
            flops=2 * rows * span * width // cheaper, bytes_accessed=moved // cheaper, transcendentals=0 if hidden is None else rows * width // 2
        ),
    )(*operands)
    return found if sends else found[0]


def after(value, earlier):
    return lax.optimization_barrier((value, earlier))


def shards(tile, tokens, block_weights, low_in, low_out):
    rows = tokens.shape[0]
    count = lax.axis_size("feat")
    cut = rows * FIRST_ROWS // 64
    head, mid = rows * HEAD_ROWS // 64, rows * SECOND_ROWS // 64
    mix = functools.partial(product, tile, weights=block_weights)

    early_rows = lax.slice_in_dim(tokens, 0, cut)
    near_early = from_partner(early_rows, "feat", BIT_A)
    late_rows, _ = after(lax.slice_in_dim(tokens, cut, rows), early_rows)
    far_late = from_partner(late_rows, "feat", BIT_B)
    tokens, late_rows = after(tokens, late_rows)
    far_head = from_partner(lax.slice_in_dim(tokens, 0, head), "feat", BIT_B)
    partial = jnp.dot(tokens, low_in, preferred_element_type=jnp.float32)
    late_rows, partial = after(late_rows, partial)
    near_late = from_partner(late_rows, "feat", BIT_A)

    sides = [[i for i in range(count) if (i >> BIT_B & 1) == side] for side in range(2)]
    latent = lax.psum_scatter(partial, "feat", scatter_dimension=0, axis_index_groups=sides, tiled=True)

    total, held_a, held_b = mix([([tokens], 0)], sends=[(head, mid - head), (mid, cut - mid)])
    (latent, near_early), total = after((latent, near_early), total)
    across = from_partner(latent, "feat", BIT_B)

    total = mix([([near_early], 1)], total=total, cheaper=1000)
    (across, near_late, far_head, held_a, held_b), total = after((across, near_late, far_head, held_a, held_b), total)
    latent = (latent + across).astype(jnp.bfloat16)
    held_a, latent = after(held_a, latent)
    far_a = from_partner(held_a, "feat", BIT_B)
    latent = lax.all_gather(latent, "feat", axis=0, axis_index_groups=sides, tiled=True)

    total = mix([([near_late], 1)], total=total, total_at=cut, cheaper=16)
    (latent, held_b), total = after((latent, held_b), total)
    far_b = from_partner(held_b, "feat", BIT_B)

    hidden = mix([([far_late], 2)], low=(latent, cut, low_out), total=total, total_at=cut, hidden=(rows, cut, None), cheaper=16)
    hidden = mix([([far_head, far_a], 2)], low=(latent, 0, low_out), total=total, hidden=(rows, 0, hidden))
    return mix([([far_b], 2)], low=(latent, mid, low_out), total=total, total_at=mid, hidden=(rows, mid, hidden))


def solution(mesh):
    in_specs = (
        P(("groups", "dp"), "feat"),
        P("feat", None, None),
        P("feat", None),
        P(None, "feat"),
    )
    out_specs = P(("groups", "dp"), "feat")

    def hidden(tokens, block_weights, low_in, low_out):
        count = mesh.shape["feat"]
        rows = tokens.shape[0] // (mesh.shape["groups"] * mesh.shape["dp"])
        half_width = block_weights.shape[2] // 2
        tile = next((t for t in (512, 256, 128) if half_width % t == 0), 0)
        fits = tile and rows % 1024 == 0 and rows <= 2048 and block_weights.shape[1] <= 2048 and block_weights.shape[1] % 128 == 0
        fits = fits and count & (count - 1) == 0 and count > 1 << BIT_B and rows % count == 0 and BIT_A < BIT_B and low_in.shape[1] % 128 == 0
        body = functools.partial(shards, tile) if fits else plain
        return jax.shard_map(body, mesh=mesh, in_specs=in_specs, out_specs=out_specs, check_vma=False)(
            tokens, block_weights, low_in, low_out
        )

    return hidden
```
